32 devices in a mesh: section: 2 (over core), ctx: 4 (over y, x), tensor: 4 (over z).
Axes of the slice: x: 2, y: 2, z: 4, core: 2. Of those that a mesh axis runs over, the one named last changes fastest.
Arguments:
- block_input: bfloat16 [2, 1024, 2048], P(None, 'ctx', 'tensor'), may hold values from -6 to 6
- out_cotangent: bfloat16 [2, 1024, 2048], P(None, 'ctx', 'tensor'), may hold values from -6 to 6
- doc_lengths: int32 [2, 6], replicated, may hold values from 200 to 2000, as said below
- norm_gain: bfloat16 [2, 2, 2048], P('section', None, 'tensor'), may hold values from 0.5 to 1.5
- norm_bias: bfloat16 [2, 2, 2048], P('section', None, 'tensor'), may hold values from -3 to 3
- qkv_weight: bfloat16 [2, 2048, 3, 2048], P('section', 'ctx', None, 'tensor'), may hold values from -0.125 to 0.125
- qkv_bias: bfloat16 [2, 3, 2048], P('section', None, 'tensor'), may hold values from -3 to 3
- out_weight: bfloat16 [2, 2048, 2048], P('section', 'tensor', 'ctx'), may hold values from -0.25 to 0.25
- out_bias: bfloat16 [2, 2048], P('section', 'tensor'), may hold values from -3 to 3
- up_weight: bfloat16 [2, 2048, 8192], P('section', 'ctx', 'tensor'), may hold values from -0.125 to 0.125
- up_bias: bfloat16 [2, 8192], P('section', 'tensor'), may hold values from -3 to 3
- down_weight: bfloat16 [2, 8192, 2048], P('section', 'tensor', 'ctx'), may hold values from -0.0625 to 0.0625
- down_bias: bfloat16 [2, 2048], P('section', 'tensor'), may hold values from -3 to 3
Outputs:
- hidden_states: bfloat16 [2, 2, 1024, 2048], P('section', None, 'ctx', 'tensor')
- input_grads: bfloat16 [2, 2, 1024, 2048], P('section', None, 'ctx', 'tensor')
- norm_gain_grad: float32 [2, 2, 2048], P('section', None, 'tensor')
- norm_bias_grad: float32 [2, 2, 2048], P('section', None, 'tensor')
- qkv_weight_grad: float32 [2, 2048, 3, 2048], P('section', 'ctx', None, 'tensor')
- qkv_bias_grad: float32 [2, 3, 2048], P('section', None, 'tensor')
- out_weight_grad: float32 [2, 2048, 2048], P('section', 'tensor', 'ctx')
- out_bias_grad: float32 [2, 2048], P('section', 'tensor')
- up_weight_grad: float32 [2, 2048, 8192], P('section', 'ctx', 'tensor')
- up_bias_grad: float32 [2, 8192], P('section', 'tensor')
- down_weight_grad: float32 [2, 8192, 2048], P('section', 'tensor', 'ctx')
- down_bias_grad: float32 [2, 2048], P('section', 'tensor')
The draws below stay inside these ranges and needn't reach their ends.
Inputs may be any that keep to these rules, and one draw needn't show every extreme that they name: `doc_lengths`: in each row, documents follow one another from position 0 with these lengths; the last ones may run past the sequence. In one micro-batch, drawn from the seed, the first length is 1024, so one document covers the whole sequence.
All inputs are finite; a program needn't handle non-finite values.
Results may differ from the reference program's by a relative error of at most 0.018.
Values may be sent and summed in bfloat16 or wider, within the bound.
No kernel may reach another device: no remote copies, remote signals or barrier semaphores. Data moves between devices by JAX's collectives and lax.ppermute only.
A program may use at most 256 MiB of HBM per device.

```python
import math
import jax
import jax.numpy as jnp
from jax import lax

D = 2048
HEADS = 8
FF = 8192
ROT = 64
MB = 2
DOC_LO = 200
DOC_HI = 2000
HD = 256
LAYERS = 2
SEQ = 1024
DOCS = 6


def draw_doc_lengths(key, part):
    key = jax.random.fold_in(key, 7)
    key_lengths, key_spanning = jax.random.split(key)
    lengths = jax.random.randint(key_lengths, (MB, DOCS), DOC_LO, DOC_HI + 1, dtype=jnp.int32)
    column = jnp.arange(DOCS, dtype=jnp.int32)
    lengths = jnp.where(column[None, :] == DOCS - 1, DOC_LO, lengths)
    lengths = jnp.where(column[None, :] == DOCS - 2, DOC_HI, lengths)
    spanning = jax.random.randint(key_spanning, (), 0, MB, dtype=jnp.int32)
    span_mask = (jnp.arange(MB, dtype=jnp.int32)[:, None] == spanning) & (column[None, :] == 0)
    return jnp.where(span_mask, SEQ, lengths).astype(jnp.int32)


def block_scale(stream_key, shape, cuts, low, largest):
    factor_of = 1.0
    for position, blocks in cuts:
        steps = jax.random.uniform(jax.random.fold_in(jax.random.fold_in(stream_key, 6), position), (blocks,), jnp.float32, low / len(cuts), largest / len(cuts))
        factor_of = factor_of * jnp.repeat(jnp.exp(steps), shape[position] // blocks).reshape((-1,) + (1,) * (len(shape) - 1 - position))
    return factor_of


def scatter_about(stream_key, extent, width, reach, shards=(), kind=jnp.bfloat16):
    values = width * jax.random.normal(stream_key, extent, jnp.float32)
    if shards:
        values = values * block_scale(stream_key, extent, shards, -0.22, 0.18)
    return jnp.clip(values, -reach, reach).astype(kind)


def setup_inputs(seed: int = 0) -> dict:
    arg_keys = jax.random.split(jax.random.key(seed), 14)
    return {
        "block_input": scatter_about(arg_keys[0], (MB, SEQ, D), 1.0, 6.0, ((1, 4), (2, 4))),
        "out_cotangent": scatter_about(arg_keys[1], (MB, SEQ, D), 1.0, 6.0, ((1, 4), (2, 4))),
        "doc_lengths": draw_doc_lengths(jax.random.fold_in(arg_keys[13], 71), 0),
        "norm_gain": jnp.clip(1.0 + 0.1 * jax.random.normal(arg_keys[3], (LAYERS, 2, D), jnp.float32), 0.5, 1.5).astype(jnp.bfloat16),
        "norm_bias": scatter_about(arg_keys[4], (LAYERS, 2, D), 0.5, 3.0, ((0, 2), (2, 4))),
        "qkv_weight": scatter_about(arg_keys[5], (LAYERS, D, 3, D), D ** -0.5, 0.125, ((0, 2), (1, 4), (3, 4))),
        "qkv_bias": scatter_about(arg_keys[6], (LAYERS, 3, D), 0.5, 3.0, ((0, 2), (2, 4))),
        "out_weight": scatter_about(arg_keys[7], (LAYERS, D, D), (D // 4) ** -0.5, 0.25, ((0, 2), (1, 4), (2, 4))),
        "out_bias": scatter_about(arg_keys[8], (LAYERS, D), 0.5, 3.0, ((0, 2), (1, 4))),
        "up_weight": scatter_about(arg_keys[9], (LAYERS, D, FF), D ** -0.5, 0.125, ((0, 2), (1, 4), (2, 4))),
        "up_bias": scatter_about(arg_keys[10], (LAYERS, FF), 0.5, 3.0, ((0, 2), (1, 4))),
        "down_weight": scatter_about(arg_keys[11], (LAYERS, FF, D), FF ** -0.5, 0.0625, ((0, 2), (1, 4), (2, 4))),
        "down_bias": scatter_about(arg_keys[12], (LAYERS, D), 0.5, 3.0, ((0, 2), (1, 4))),
    }


EPSILON = 1e-05
PRECISE = lax.Precision.HIGHEST

@jax.custom_vjp
def low(v):
    return lax.optimization_barrier(v.astype(jnp.bfloat16)).astype(jnp.float32)

@jax.custom_vjp
def low_back(v):
    return v

def low_keep(v):
    return (low(v), None)

def low_pass(kept, grad):
    return (grad,)

def back_keep(v):
    return (v, None)

def back_low(kept, grad):
    return (low(grad),)
low.defvjp(low_keep, low_pass)
low_back.defvjp(back_keep, back_low)

def doc_layout(lengths, positions):
    doc_ends = jnp.cumsum(lengths).astype(jnp.int32)
    passed = doc_ends[None, :] <= positions[:, None]
    segment = lax.optimization_barrier(jnp.sum(passed.astype(jnp.int32), axis=1)).astype(jnp.int32)
    begins = lax.optimization_barrier(jnp.max(jnp.where(passed, doc_ends[None, :], 0), axis=1)).astype(jnp.int32)
    return (segment, (positions - begins).astype(jnp.int32))

def rotary_tables(positions, rot_dims):
    inverse = 10000.0 ** (-jnp.arange(0, rot_dims, 2, dtype=jnp.float32) / rot_dims)
    angles = positions.astype(jnp.float32)[:, None] * inverse[None, :]
    return (jnp.cos(angles)[:, None, :], jnp.sin(angles)[:, None, :])

def rotate(field, cosine_table, sine_table):
    half_rot = cosine_table.shape[-1]
    front_half = field[..., :half_rot]
    back_half = field[..., half_rot:2 * half_rot]
    return jnp.concatenate([front_half * cosine_table - back_half * sine_table, back_half * cosine_table + front_half * sine_table, field[..., 2 * half_rot:]], axis=-1)

def layer_norm(values, gain_row, bias_row):
    centered = values - lax.optimization_barrier(jnp.mean(values, axis=-1, keepdims=True))
    variance = lax.optimization_barrier(jnp.mean(centered * centered, axis=-1, keepdims=True))
    return centered * lax.rsqrt(variance + EPSILON) * gain_row + bias_row

def attention(queries, keys_rot, values_h, segment, positions):
    block_rows = math.gcd(SEQ, 512)
    block_count = SEQ // block_rows

    def attend_block(inputs):
        query_block, query_pos, query_seg = inputs
        scores = low_back(jnp.einsum('qhd,khd->qhk', query_block, keys_rot, precision=PRECISE) * HD ** (-0.5))
        allowed = ((positions[None, :] <= query_pos[:, None]) & (segment[None, :] == query_seg[:, None]))[:, None, :]
        masked = jnp.where(allowed, scores, -1e+30)
        peak = lax.optimization_barrier(jnp.max(masked, axis=-1, keepdims=True))
        exponent = jnp.where(allowed, jnp.exp(masked - peak), 0.0)
        probability = exponent / lax.optimization_barrier(jnp.sum(exponent, axis=-1, keepdims=True))
        return jnp.einsum('qhk,khd->qhd', low(probability), values_h, precision=PRECISE)
    outputs = lax.map(jax.checkpoint(attend_block), (queries.reshape(block_count, block_rows, HEADS, HD), positions.reshape(block_count, block_rows), segment.reshape(block_count, block_rows)))
    return outputs.reshape(SEQ, HEADS, HD)

def layer(values, weights, cosine_table, sine_table, segment, positions):
    gains, biases, w_qkv, b_qkv, w_out, b_out, w_up, b_up, w_down, b_down = weights
    norm_one = low(layer_norm(values, gains[0], biases[0]))
    norm_two = low(layer_norm(values, gains[1], biases[1]))
    mixture = low_back(jnp.dot(norm_one, w_qkv.reshape(D, 3 * D), precision=PRECISE) + b_qkv.reshape(3 * D))
    mixture = mixture.reshape(SEQ, 3, HEADS, HD)
    queries = low(rotate(mixture[:, 0], cosine_table, sine_table))
    keys_rot = low(rotate(mixture[:, 1], cosine_table, sine_table))
    values_h = low(mixture[:, 2])
    attended = attention(queries, keys_rot, values_h, segment, positions)
    attended = low(low_back(attended)).reshape(SEQ, D)
    pre_up = low_back(jnp.dot(norm_two, w_up, precision=PRECISE) + b_up)
    activated = low(jax.nn.gelu(pre_up, approximate=False))
    return values + jnp.dot(attended, w_out, precision=PRECISE) + b_out + jnp.dot(activated, w_down, precision=PRECISE) + b_down

def reference(block_input, out_cotangent, doc_lengths, norm_gain, norm_bias, qkv_weight, qkv_bias, out_weight, out_bias, up_weight, up_bias, down_weight, down_bias):
    params = tuple((a.astype(jnp.float32) for a in (norm_gain, norm_bias, qkv_weight, qkv_bias, out_weight, out_bias, up_weight, up_bias, down_weight, down_bias)))
    positions = jnp.arange(SEQ, dtype=jnp.int32)

    def micro_step(totals, inputs):
        current, cotangent, lengths = inputs
        segment, doc_pos = doc_layout(lengths, positions)
        cosine_table, sine_table = rotary_tables(doc_pos, ROT)

        def apply_layer(values, weights):
            return layer(values, weights, cosine_table, sine_table, segment, positions)
        pullbacks = []
        states = []
        for layer_id in range(LAYERS):
            weights = tuple((p[layer_id] for p in params))
            result, pullback = jax.vjp(apply_layer, current, weights)
            current = low(result)
            states.append(current)
            pullbacks.append(pullback)
        upstream = cotangent
        in_grads = [None] * LAYERS
        per_layer = [None] * LAYERS
        for layer_id in reversed(range(LAYERS)):
            grad_value, grad_weights = pullbacks[layer_id](upstream)
            upstream = low(grad_value)
            in_grads[layer_id] = upstream
            per_layer[layer_id] = grad_weights
        totals = tuple((a + jnp.stack([per_layer[j][i] for j in range(LAYERS)]) for i, a in enumerate(totals)))
        return (totals, (jnp.stack(states), jnp.stack(in_grads)))
    zeros_init = tuple((jnp.zeros_like(p) for p in params))
    grads, (states, in_grads) = lax.scan(micro_step, zeros_init, (block_input.astype(jnp.float32), out_cotangent.astype(jnp.float32), doc_lengths))
    hidden_states = jnp.swapaxes(states, 0, 1).astype(jnp.bfloat16)
    input_grads = jnp.swapaxes(in_grads, 0, 1).astype(jnp.bfloat16)
    return (hidden_states, input_grads, grads[0], grads[1], grads[2], grads[3], grads[4], grads[5], grads[6], grads[7], grads[8], grads[9])
```

```python
import functools
import math

import jax
import jax.numpy as jnp
from jax import lax
from jax.experimental import pallas as pl
from jax.experimental.pallas import tpu as pltpu
from jax.sharding import PartitionSpec as P

ROT = 64
HD = 256


EPSILON = 1e-05


def passed_along(value, axis, steps):
    count = lax.axis_size(axis)
    initial, last = (max(0, -steps), min(count, count - steps))
    return lax.ppermute(value, axis, [(source, source + steps) for source in range(initial, last)])


def doc_layout(lengths, positions):
    doc_ends = jnp.cumsum(lengths)
    passed = doc_ends[None, :] <= positions[:, None]
    segment = jnp.sum(passed.astype(jnp.int32), axis=1)
    begins = jnp.max(jnp.where(passed, doc_ends[None, :], 0), axis=1)
    return (segment, positions - begins)


def rotary_tables(positions, rot_dims):
    inverse = 10000.0 ** (-jnp.arange(0, rot_dims, 2, dtype=jnp.float32) / rot_dims)
    angles = positions.astype(jnp.float32)[:, None] * inverse[None, :]
    return (jnp.cos(angles)[:, None, :], jnp.sin(angles)[:, None, :])


def rotate(field, cosine_table, sine_table):
    half_rot = cosine_table.shape[-1]
    front_half = field[..., :half_rot]
    back_half = field[..., half_rot : 2 * half_rot]
    return jnp.concatenate(
        [
            front_half * cosine_table - back_half * sine_table,
            back_half * cosine_table + front_half * sine_table,
            field[..., 2 * half_rot :],
        ],
        axis=-1,
    )


def unrotate(grad_field, cosine_table, sine_table):
    half_rot = cosine_table.shape[-1]
    front_half = grad_field[..., :half_rot]
    back_half = grad_field[..., half_rot : 2 * half_rot]
    return jnp.concatenate(
        [
            front_half * cosine_table + back_half * sine_table,
            back_half * cosine_table - front_half * sine_table,
            grad_field[..., 2 * half_rot :],
        ],
        axis=-1,
    )


def normalize(values, gain_row, bias_row):
    centered = values - jnp.mean(values, axis=-1, keepdims=True)
    variance = jnp.mean(centered * centered, axis=-1, keepdims=True)
    inv_std = lax.rsqrt(variance + EPSILON)
    normed = centered * inv_std
    return (normed * gain_row + bias_row, normed, inv_std)


def norm_backward(grad_norm, normed, inv_std, gain_row):
    scaled = grad_norm * gain_row
    return inv_std * (
        scaled
        - jnp.mean(scaled, axis=-1, keepdims=True)
        - normed * jnp.mean(scaled * normed, axis=-1, keepdims=True)
    )


def gelu_exact(values):
    return jax.nn.gelu(values, approximate=False)


def pair_grads(
    queries,
    grad_rows,
    log_mass,
    row_delta,
    query_pos,
    query_seg,
    key_tile,
    value_tile,
    key_pos,
    key_seg,
    scaling,
):
    scores = (
        jnp.einsum("qhd,khd->qhk", queries, key_tile, preferred_element_type=jnp.float32) * scaling
    )
    allowed = ((key_pos[None, :] <= query_pos[:, None]) & (key_seg[None, :] == query_seg[:, None]))[
        :, None, :
    ]
    probability = jnp.where(allowed, jnp.exp(scores - log_mass[..., None]), 0.0)
    grad_prob = jnp.einsum(
        "qhd,khd->qhk", grad_rows, value_tile, preferred_element_type=jnp.float32
    )
    grad_score = (probability * (grad_prob - row_delta[..., None])).astype(jnp.bfloat16)
    grad_query = None
    grad_key = None
    grad_value = None
    grad_query = (
        jnp.einsum("qhk,khd->qhd", grad_score, key_tile, preferred_element_type=jnp.float32)
        * scaling
    )
    grad_key = (
        jnp.einsum("qhk,qhd->khd", grad_score, queries, preferred_element_type=jnp.float32)
        * scaling
    )
    grad_value = jnp.einsum(
        "qhk,qhd->khd",
        probability.astype(jnp.bfloat16),
        grad_rows,
        preferred_element_type=jnp.float32,
    )
    return (grad_query, grad_key, grad_value)


def put_slot(buffer, slot_id, is_valid, fresh):
    former = lax.dynamic_index_in_dim(buffer, slot_id, 0, keepdims=False)
    return lax.dynamic_update_index_in_dim(buffer, jnp.where(is_valid, fresh, former), slot_id, 0)


def shards(
    block_input,
    out_cotangent,
    doc_lengths,
    norm_gain,
    norm_bias,
    qkv_weight,
    qkv_bias,
    out_weight,
    out_bias,
    up_weight,
    up_bias,
    down_weight,
    down_bias,
):
    section_count = lax.axis_size("section")
    section_id = lax.axis_index("section")
    ctx_count = lax.axis_size("ctx")
    ctx_id = lax.axis_index("ctx")
    tensor_id = lax.axis_index("tensor")
    micro_count, row_count, shard_width = block_input.shape
    seq_len = row_count * ctx_count
    w_qkv, w_up, w_out, w_down = (
        lax.all_gather(qkv_weight[0], "ctx", axis=0, tiled=True),
        lax.all_gather(up_weight[0], "ctx", axis=0, tiled=True),
        lax.all_gather(out_weight[0], "ctx", axis=1, tiled=True),
        lax.all_gather(down_weight[0], "ctx", axis=1, tiled=True),
    )
    model_width = w_qkv.shape[0]
    local_width = w_qkv.shape[2]
    head_count = local_width // HD
    hidden = w_up.shape[1]
    w_qkv_flat = w_qkv.reshape(model_width, 3 * local_width)
    bias_qkv = qkv_bias[0].astype(jnp.float32).reshape(3 * local_width)
    bias_up = up_bias[0].astype(jnp.float32)
    bias_sum = out_bias[0].astype(jnp.float32) + down_bias[0].astype(jnp.float32)
    gain_local = norm_gain[0]
    bias_local = norm_bias[0]
    row_index = ctx_id * row_count + jnp.arange(row_count, dtype=jnp.int32)
    key_index = jnp.arange(seq_len, dtype=jnp.int32)
    scaling = HD ** (-0.5)
    group_size = ctx_count
    while group_size > 1 and (row_count * group_size > 2048 or ctx_count % group_size):
        group_size -= 1
    tile_rows = row_count * group_size
    tile_count = seq_len // tile_rows

    def layout(slot_id):
        lengths = lax.dynamic_index_in_dim(doc_lengths, slot_id, 0, keepdims=False)
        key_seg, key_pos = doc_layout(lengths, key_index)
        query_seg = lax.dynamic_slice_in_dim(key_seg, ctx_id * row_count, row_count)
        query_pos = lax.dynamic_slice_in_dim(key_pos, ctx_id * row_count, row_count)
        cosine_table, sine_table = rotary_tables(query_pos, ROT)
        return (key_seg, query_seg, cosine_table, sine_table)

    def prepare(gathered, gain_full, bias_full, cosine_table, sine_table):
        values = gathered.astype(jnp.float32)
        gains = gain_full.astype(jnp.float32)
        biases = bias_full.astype(jnp.float32)
        norm_one, normed_one, inv_one = normalize(values, gains[0], biases[0])
        norm_two, normed_two, inv_two = normalize(values, gains[1], biases[1])
        norm_one = norm_one.astype(jnp.bfloat16)
        norm_two = norm_two.astype(jnp.bfloat16)
        mixture = jnp.dot(norm_one, w_qkv_flat, preferred_element_type=jnp.float32) + bias_qkv
        mixture = mixture.reshape(row_count, 3, head_count, HD)
        queries = rotate(mixture[:, 0], cosine_table, sine_table).astype(jnp.bfloat16)
        keys_rot = rotate(mixture[:, 1], cosine_table, sine_table).astype(jnp.bfloat16)
        values_h = mixture[:, 2].astype(jnp.bfloat16)
        pre_up = jnp.dot(norm_two, w_up, preferred_element_type=jnp.float32) + bias_up
        return (
            norm_one,
            normed_one,
            inv_one,
            norm_two,
            normed_two,
            inv_two,
            gains,
            queries,
            keys_rot,
            values_h,
            pre_up,
        )

    tick_count = micro_count + section_count - 1
    received = jnp.zeros((row_count, shard_width), jnp.bfloat16)
    saved_inputs = jnp.zeros((micro_count, row_count, shard_width), jnp.bfloat16)
    saved_attn = jnp.zeros((micro_count, row_count, head_count, HD), jnp.float32)
    saved_mass = jnp.zeros((micro_count, row_count, head_count), jnp.float32)
    states = jnp.zeros((micro_count, row_count, shard_width), jnp.bfloat16)
    for tick_id in range(tick_count):
        slot_raw = tick_id - section_id
        is_valid = (slot_raw >= 0) & (slot_raw < micro_count)
        slot_id = jnp.clip(slot_raw, 0, micro_count - 1)
        layer_in = jnp.where(section_id == 0, block_input[min(tick_id, micro_count - 1)], received)
        forward_key_seg, forward_query_seg, forward_cosine_table, forward_sine_table = layout(
            slot_id
        )
        forward_gathered = lax.all_gather(layer_in, "tensor", axis=1, tiled=True)
        forward_gain_full = lax.all_gather(gain_local, "tensor", axis=1, tiled=True)
        forward_bias_full = lax.all_gather(bias_local, "tensor", axis=1, tiled=True)
        prepared = prepare(
            forward_gathered,
            forward_gain_full,
            forward_bias_full,
            forward_cosine_table,
            forward_sine_table,
        )
        forward_queries = prepared[7]
        forward_keys_rot = prepared[8]
        forward_values_h = prepared[9]
        forward_pre_up = prepared[10]
        running_max = jnp.full((row_count, head_count), -1e30, jnp.float32)
        attend_key_tile = lax.all_gather(forward_keys_rot, "ctx", axis=0, tiled=True)
        attend_value_tile = lax.all_gather(forward_values_h, "ctx", axis=0, tiled=True)
        key_count = attend_key_tile.shape[0]
        attend_key_pos = jnp.arange(key_count, dtype=jnp.int32)
        allowed = (
            (attend_key_pos[None, :] <= row_index[:, None])
            & (forward_key_seg[None, :] == forward_query_seg[:, None])
        )[:, None, :]
        scores = (
            jnp.einsum(
                "qhd,khd->qhk", forward_queries, attend_key_tile, preferred_element_type=jnp.float32
            )
            * scaling
        )
        new_max = jnp.maximum(running_max, jnp.max(jnp.where(allowed, scores, -1e30), axis=-1))
        weights_tile = jnp.where(allowed, jnp.exp(scores - new_max[..., None]), 0.0)
        running_sum = jnp.sum(weights_tile, axis=-1)
        weighted = jnp.einsum(
            "qhk,khd->qhd",
            weights_tile.astype(jnp.bfloat16),
            attend_value_tile,
            preferred_element_type=jnp.float32,
        )
        weighted, running_max, running_sum = (weighted, new_max, running_sum)
        forward_attn_f = weighted / running_sum[..., None]
        forward_log_mass = running_max + jnp.log(running_sum)
        forward_attn_r = forward_attn_f.reshape(row_count, local_width).astype(jnp.bfloat16)
        forward_activated = gelu_exact(forward_pre_up).astype(jnp.bfloat16)
        partial_out = jnp.dot(forward_attn_r, w_out, preferred_element_type=jnp.float32) + jnp.dot(
            forward_activated, w_down, preferred_element_type=jnp.float32
        )
        summed = lax.psum_scatter(
            partial_out.astype(jnp.bfloat16), "tensor", scatter_dimension=1, tiled=True
        ).astype(jnp.float32)
        result = layer_in.astype(jnp.float32) + summed + bias_sum
        result, attn_f, log_mass = (result.astype(jnp.bfloat16), forward_attn_f, forward_log_mass)
        saved_inputs = put_slot(saved_inputs, slot_id, is_valid, layer_in)
        saved_attn = put_slot(saved_attn, slot_id, is_valid, attn_f)
        saved_mass = put_slot(saved_mass, slot_id, is_valid, log_mass)
        states = put_slot(states, slot_id, is_valid, result)
        if tick_id + 1 < tick_count:
            received = passed_along(result, "section", 1)
    totals = (
        jnp.zeros((2, shard_width), jnp.float32),
        jnp.zeros((2, shard_width), jnp.float32),
        jnp.zeros((model_width, 3 * local_width), jnp.float32),
        jnp.zeros((3 * local_width,), jnp.float32),
        jnp.zeros((local_width, model_width), jnp.float32),
        jnp.zeros((shard_width,), jnp.float32),
        jnp.zeros((model_width, hidden), jnp.float32),
        jnp.zeros((hidden,), jnp.float32),
        jnp.zeros((hidden, model_width), jnp.float32),
    )
    received_grad = jnp.zeros((row_count, shard_width), jnp.bfloat16)
    grads_in = jnp.zeros((micro_count, row_count, shard_width), jnp.bfloat16)
    for tick_id in range(tick_count):
        slot_raw = tick_id - (section_count - 1 - section_id)
        is_valid = (slot_raw >= 0) & (slot_raw < micro_count)
        slot_id = jnp.clip(slot_raw, 0, micro_count - 1)
        grad_out = jnp.where(
            section_id == section_count - 1,
            out_cotangent[min(tick_id, micro_count - 1)],
            received_grad,
        )
        layer_in = lax.dynamic_index_in_dim(saved_inputs, slot_id, 0, keepdims=False)
        attn_f = lax.dynamic_index_in_dim(saved_attn, slot_id, 0, keepdims=False)
        log_mass = lax.dynamic_index_in_dim(saved_mass, slot_id, 0, keepdims=False)
        backward_key_seg, backward_query_seg, backward_cosine_table, backward_sine_table = layout(
            slot_id
        )
        backward_gathered = lax.all_gather(layer_in, "tensor", axis=1, tiled=True)
        grad_full = lax.all_gather(grad_out, "tensor", axis=1, tiled=True)
        backward_gain_full = lax.all_gather(gain_local, "tensor", axis=1, tiled=True)
        backward_bias_full = lax.all_gather(bias_local, "tensor", axis=1, tiled=True)
        (
            backward_norm_one,
            backward_normed_one,
            backward_inv_one,
            backward_norm_two,
            backward_normed_two,
            backward_inv_two,
            backward_gains,
            backward_queries,
            backward_keys_rot,
            backward_values_h,
            backward_pre_up,
        ) = prepare(
            backward_gathered,
            backward_gain_full,
            backward_bias_full,
            backward_cosine_table,
            backward_sine_table,
        )
        attn_r = attn_f.reshape(row_count, local_width).astype(jnp.bfloat16)
        activated_f, gelu_pullback = jax.vjp(gelu_exact, backward_pre_up)
        activated = activated_f.astype(jnp.bfloat16)
        backward_grad_w_out = jnp.dot(attn_r.T, grad_full, preferred_element_type=jnp.float32)
        backward_grad_w_down = jnp.dot(activated.T, grad_full, preferred_element_type=jnp.float32)
        backward_grad_b_out = jnp.sum(grad_out.astype(jnp.float32), axis=0)
        grad_attn = jnp.dot(grad_full, w_out.T, preferred_element_type=jnp.float32)
        grad_act = jnp.dot(grad_full, w_down.T, preferred_element_type=jnp.float32)
        grad_attn_r = grad_attn.astype(jnp.bfloat16).reshape(row_count, head_count, HD)
        grad_up = gelu_pullback(grad_act)[0].astype(jnp.bfloat16)
        backward_grad_w_up = jnp.dot(
            backward_norm_two.T, grad_up, preferred_element_type=jnp.float32
        )
        backward_grad_b_up = jnp.sum(grad_up.astype(jnp.float32), axis=0)
        grad_norm_two = jnp.dot(grad_up, w_up.T, preferred_element_type=jnp.float32)
        row_delta = jnp.sum(grad_attn_r.astype(jnp.float32) * attn_f, axis=-1)
        key_all = lax.all_gather(backward_keys_rot, "ctx", axis=0, tiled=True)
        value_all = lax.all_gather(backward_values_h, "ctx", axis=0, tiled=True)

        def over_keys(grad_query, tile_id):
            first_key = tile_id * tile_rows
            key_tile = lax.dynamic_slice_in_dim(key_all, first_key, tile_rows)
            value_tile = lax.dynamic_slice_in_dim(value_all, first_key, tile_rows)
            key_pos = first_key + jnp.arange(tile_rows, dtype=jnp.int32)
            key_tile_seg = lax.dynamic_slice_in_dim(backward_key_seg, first_key, tile_rows)
            part_query, part_key, part_value = pair_grads(
                backward_queries,
                grad_attn_r,
                log_mass,
                row_delta,
                row_index,
                backward_query_seg,
                key_tile,
                value_tile,
                key_pos,
                key_tile_seg,
                scaling,
            )
            return (grad_query + part_query, (part_key, part_value))

        backward_tiles = jnp.arange(tile_count, dtype=jnp.int32)
        zero_rows = jnp.zeros((row_count, head_count, HD), jnp.float32)
        grad_query, (tiles_key, tiles_value) = lax.scan(
            lambda c, t: over_keys(c, t), zero_rows, backward_tiles
        )
        grad_key = lax.psum_scatter(
            tiles_key.reshape(seq_len, head_count, HD).astype(jnp.bfloat16),
            "ctx",
            scatter_dimension=0,
            tiled=True,
        ).astype(jnp.float32)
        grad_value = lax.psum_scatter(
            tiles_value.reshape(seq_len, head_count, HD).astype(jnp.bfloat16),
            "ctx",
            scatter_dimension=0,
            tiled=True,
        ).astype(jnp.float32)
        grad_mixture = jnp.stack(
            [
                unrotate(grad_query, backward_cosine_table, backward_sine_table),
                unrotate(grad_key, backward_cosine_table, backward_sine_table),
                grad_value,
            ],
            axis=1,
        )
        grad_mixture = grad_mixture.reshape(row_count, 3 * local_width).astype(jnp.bfloat16)
        backward_grad_w_qkv = jnp.dot(
            backward_norm_one.T, grad_mixture, preferred_element_type=jnp.float32
        )
        backward_grad_b_qkv = jnp.sum(grad_mixture.astype(jnp.float32), axis=0)
        grad_norm_one = jnp.dot(grad_mixture, w_qkv_flat.T, preferred_element_type=jnp.float32)
        feature_start = tensor_id * shard_width
        whole_one = lax.psum(grad_norm_one.astype(jnp.bfloat16), "tensor").astype(jnp.float32)
        whole_two = lax.psum(grad_norm_two.astype(jnp.bfloat16), "tensor").astype(jnp.float32)
        grad_input = norm_backward(
            whole_one, backward_normed_one, backward_inv_one, backward_gains[0]
        ) + norm_backward(whole_two, backward_normed_two, backward_inv_two, backward_gains[1])
        grad_input = lax.dynamic_slice_in_dim(grad_input, feature_start, shard_width, 1)
        backward_gain_terms = jnp.stack(
            [
                jnp.sum(whole_one * backward_normed_one, axis=0),
                jnp.sum(whole_two * backward_normed_two, axis=0),
            ]
        )
        backward_bias_terms = jnp.stack([jnp.sum(whole_one, axis=0), jnp.sum(whole_two, axis=0)])
        backward_gain_terms = lax.dynamic_slice_in_dim(
            backward_gain_terms, feature_start, shard_width, 1
        )
        backward_bias_terms = lax.dynamic_slice_in_dim(
            backward_bias_terms, feature_start, shard_width, 1
        )
        result_grad = (grad_out.astype(jnp.float32) + grad_input).astype(jnp.bfloat16)
        terms = (
            backward_gain_terms,
            backward_bias_terms,
            backward_grad_w_qkv,
            backward_grad_b_qkv,
            backward_grad_w_out,
            backward_grad_b_out,
            backward_grad_w_up,
            backward_grad_b_up,
            backward_grad_w_down,
        )
        keep_mask = is_valid.astype(jnp.float32)
        totals = jax.tree.map(lambda a, g: a + keep_mask * g, totals, terms)
        grads_in = put_slot(grads_in, slot_id, is_valid, result_grad)
        if tick_id + 1 < tick_count:
            received_grad = passed_along(result_grad, "section", -1)
    (
        gain_terms,
        bias_terms,
        grad_w_qkv,
        grad_b_qkv,
        grad_w_out,
        grad_b_out,
        grad_w_up,
        grad_b_up,
        grad_w_down,
    ) = totals
    shard_qkv, shard_up, shard_out, shard_down = (
        lax.psum_scatter(
            grad_w_qkv.reshape(model_width, 3, local_width).astype(jnp.bfloat16),
            "ctx",
            scatter_dimension=0,
            tiled=True,
        ).astype(jnp.float32),
        lax.psum_scatter(
            grad_w_up.astype(jnp.bfloat16), "ctx", scatter_dimension=0, tiled=True
        ).astype(jnp.float32),
        lax.psum_scatter(
            grad_w_out.astype(jnp.bfloat16), "ctx", scatter_dimension=1, tiled=True
        ).astype(jnp.float32),
        lax.psum_scatter(
            grad_w_down.astype(jnp.bfloat16), "ctx", scatter_dimension=1, tiled=True
        ).astype(jnp.float32),
    )
    gain_sum, bias_sum_grad, qkv_bias_sum, up_bias_sum, out_bias_sum = lax.psum(
        (gain_terms, bias_terms, grad_b_qkv, grad_b_up, grad_b_out), "ctx"
    )
    return (
        states[None],
        grads_in[None],
        gain_sum[None],
        bias_sum_grad[None],
        shard_qkv[None],
        qkv_bias_sum.reshape(3, local_width)[None],
        shard_out[None],
        out_bias_sum[None],
        shard_up[None],
        up_bias_sum[None],
        shard_down[None],
        out_bias_sum[None],
    )


AXES = ("section", "y", "x", "tensor")
F32, BF16 = jnp.float32, jnp.bfloat16
ROWS = 256
WIDTH = 512
MODEL = 2048
HID = 1024
A_ROWS = 3 * 256
U_ROWS = 4 * 256
O_ROWS = 2 * 128 + 2 * 512
ANY = pl.BlockSpec(memory_space=pl.ANY)
VMEM = pl.BlockSpec(memory_space=pltpu.VMEM)
SMEM = pl.BlockSpec(memory_space=pltpu.SMEM)


def across(value, axis, bits):
    count = lax.axis_size(axis)
    return lax.ppermute(value, axis, [(i, i ^ bits) for i in range(count)])


def pick(value, index, axis=0):
    return lax.dynamic_index_in_dim(value, index, axis, keepdims=False)


def in_order(mine, theirs, bit, axis=0):
    return jnp.where(
        bit == 0, jnp.stack([mine, theirs], axis), jnp.stack([theirs, mine], axis)
    )


def routed(value, route):
    pairs = []
    for s in range(2):
        for c in range(4):
            for z in range(4):
                ts, ty, tx, tz = route(s, c // 2, c % 2, z)
                pairs.append(((s * 4 + c) * 4 + z, (ts * 4 + 2 * ty + tx) * 4 + tz))
    return lax.ppermute(value, AXES, pairs)


def dot_nn(a, b):
    return lax.dot_general(a, b, (((1,), (0,)), ((), ())), preferred_element_type=F32)


def dot_nt(a, b):
    return lax.dot_general(a, b, (((1,), (1,)), ((), ())), preferred_element_type=F32)


def dot_tn(a, b):
    return lax.dot_general(a, b, (((0,), (0,)), ((), ())), preferred_element_type=F32)


def call(body, name, ins, in_specs, outs, out_specs, scratch, limit=48):
    return pl.pallas_call(
        body,
        out_shape=[jax.ShapeDtypeStruct(shape, dtype) for shape, dtype in outs],
        in_specs=in_specs,
        out_specs=out_specs,
        scratch_shapes=scratch,
        name=name,
        cost_estimate=pl.CostEstimate(flops=1, bytes_accessed=1, transcendentals=0),
        compiler_params=pltpu.CompilerParams(vmem_limit_bytes=limit * 2**20),
    )(*ins)


class Copies:
    def __init__(self, sems):
        self.sems = sems
        self.count = 0

    def start(self, source, target):
        copy = pltpu.make_async_copy(source, target, self.sems.at[self.count])
        self.count += 1
        copy.start()
        return copy


def finish(copies):
    for copy in copies:
        copy.wait()


def span(index, size):
    return pl.ds(pl.multiple_of(index * size, size), size)


def place_pieces(copies, pieces, target, idx):
    x, z = idx[2], idx[3]
    made = []
    for n, piece in enumerate(pieces):
        row = x if n < 4 else 1 - x
        made.append(
            copies.start(piece, target.at[span(row, ROWS), span(z ^ (n % 4), WIDTH)])
        )
    return made


def piece_places(idx):
    s, c = idx[0], 2 * idx[1] + idx[2]
    return [(c ^ (n % 4), s ^ (n // 4)) for n in range(8)]


def place_qkv(copies, pieces, base, target, idx):
    made = []
    for (c, k), piece in zip(piece_places(idx), pieces):
        for t in range(3):
            made.append(
                copies.start(
                    piece.at[pl.ds(base + t * 256, 256)],
                    target.at[span(2 * c + k, 256), pl.ds(t * 256, 256)],
                )
            )
    return made


def place_up(copies, pieces, base, target, idx):
    made = []
    for u in range(4):
        made.append([])
        for (c, k), piece in zip(piece_places(idx), pieces):
            made[-1].append(
                copies.start(
                    piece.at[pl.ds(base + u * 256, 256)],
                    target.at[span(2 * c + k, 256), pl.ds(u * 256, 256)],
                )
            )
    return made


def place_inner(copies, pieces, base, target, idx):
    made = []
    for (c, k), piece in zip(piece_places(idx), pieces):
        for half in range(2):
            cols = span(2 * c + half, 256)
            made.append(
                copies.start(
                    piece.at[pl.ds(base + half * 128, 128)], target.at[span(k, 128), cols]
                )
            )
            made.append(
                copies.start(
                    piece.at[pl.ds(base + 256 + half * 512, 512)],
                    target.at[pl.ds(pl.multiple_of(256 + k * 512, 256), 512), cols],
                )
            )
    return made


def prepare_a_body(idx, qkv, own, send):
    s, x = idx[0], idx[2]
    for k, to in ((1 - s, send), (s, own)):
        for side, xx in ((0, x), (1, 1 - x)):
            for t in range(3):
                to[side, t * 256 : (t + 1) * 256, :] = qkv[t, span(k, 256), span(xx, 256)]


def prepare_f_body(idx, out, up, down, u_own, u_send, o_own, o_send):
    s, x = idx[0], idx[2]
    for k, u_to, o_to in ((1 - s, u_send, o_send), (s, u_own, o_own)):
        for side, xx in ((0, x), (1, 1 - x)):
            for u in range(4):
                u_to[side, u * 256 : (u + 1) * 256, :] = up[span(k, 256), span(xx * 4 + u, 256)]
            for half in range(2):
                cols = slice(half * 256, half * 256 + 256)
                o_to[side, half * 128 : half * 128 + 128, :] = out[span(2 * xx + k, 128), cols]
                o_to[side, 256 + half * 512 : 768 + half * 512, :] = down[
                    span(2 * xx + k, 512), cols
                ]


def turn(block, tables, sign):
    cosine, front, back = tables
    return (
        block * cosine
        + sign * (pltpu.roll(block, 96, 1) * front + pltpu.roll(block, 32, 1) * back)
    )


def norm_body(base, idx, *refs):
    pieces, weights = refs[:8], refs[8:16]
    wide, bias, cosine, front, back = refs[16:21]
    n_zero, n_one, xhat, q, kv, x_piece, inv_all = refs[21:28]
    block_in, w, sems = refs[28:]
    copies = Copies(sems)
    loads = place_pieces(copies, pieces, block_in, idx)
    fills = place_qkv(copies, weights, base, w, idx)
    finish(loads)
    step = 32

    def rows_of(i, carry):
        rows = pl.ds(pl.multiple_of(i * step, step), step)
        values = block_in[rows, :].astype(F32)
        centered = values - jnp.mean(values, axis=1, keepdims=True)
        inv = lax.rsqrt(jnp.mean(centered * centered, axis=1, keepdims=True) + EPSILON)
        normed = centered * inv
        xhat[rows, :] = normed.astype(BF16)
        n_zero[rows, :] = (normed * wide[0:1, :] + wide[2:3, :]).astype(BF16)
        n_one[rows, :] = (normed * wide[1:2, :] + wide[3:4, :]).astype(BF16)
        inv_all[rows, :] = jnp.broadcast_to(inv, (step, 128))
        return carry

    lax.fori_loop(0, 2 * ROWS // step, rows_of, 0)
    finish(fills)
    for half in range(2):
        rows = pl.ds(half * ROWS, ROWS)
        tables = (cosine[rows, :], front[rows, :], back[rows, :])
        for t in range(3):
            cols = pl.ds(t * 256, 256)
            mixed = dot_nn(n_zero[rows, :], w[:, cols]) + bias[0:1, cols]
            if t < 2:
                turned = turn(mixed[:, :128], tables, 1.0).astype(BF16)
                rest = mixed[:, 128:].astype(BF16)
                if t == 0:
                    q[rows, 0:128] = turned
                    q[rows, 128:256] = rest
                else:
                    kv[rows, 0:128] = turned
                    kv[rows, 128:256] = rest
            else:
                kv[rows, 256:512] = mixed.astype(BF16)
    x_piece[...] = xhat[span(idx[2], ROWS), span(idx[3], WIDTH)]


def up_body(base, idx, *refs):
    weights = refs[:8]
    n_one, bias, act, slope, w, sems = refs[8:]
    fills = place_up(Copies(sems), weights, base, w, idx)
    for u in range(4):
        finish(fills[u])
        cols = pl.ds(u * 256, 256)
        for part in range(4):
            rows = pl.ds(part * 128, 128)
            value = dot_nn(n_one[rows, :], w[:, cols]) + bias[0:1, cols]
            phi = 0.5 + 0.5 * lax.erf(value * (0.5**0.5))
            act[rows, cols] = (value * phi).astype(BF16)
            slope[rows, cols] = phi + value * (
                jnp.exp(-0.5 * value * value) * (0.5 / math.pi) ** 0.5
            )


def attend_body(idx, lengths, q, kv_own, kv_other, prob, attn):
    s, y = idx[0], idx[1]
    step = 128
    for part in range(2 * ROWS // step):
        chunk = part * step // ROWS
        rows = pl.ds(part * step, step)
        first = (2 * chunk + s) * ROWS + part * step % ROWS
        q_pos = first + lax.broadcasted_iota(jnp.int32, (step, 1), 0)
        begin = jnp.zeros((step, 1), jnp.int32)
        end = 0
        for i in range(lengths.shape[1]):
            end = end + lengths[y, i]
            begin = jnp.where(q_pos >= end, end, begin)
        scores = []
        for side, kv in ((0, kv_own), (1, kv_other)):
            column = lax.broadcasted_iota(jnp.int32, (1, 2 * ROWS), 1)
            core = s if side == 0 else 1 - s
            upper = (column >= ROWS).astype(jnp.int32)
            k_pos = column + (upper + core) * ROWS
            allowed = (k_pos <= q_pos) & (k_pos >= begin)
            score = dot_nt(q[rows, :], kv[:, 0:256]) * (HD**-0.5)
            scores.append(jnp.where(allowed, score, -1e30))
        peak = jnp.maximum(
            jnp.max(scores[0], axis=1, keepdims=True), jnp.max(scores[1], axis=1, keepdims=True)
        )
        masses = [jnp.exp(score - peak) for score in scores]
        total = jnp.sum(masses[0], axis=1, keepdims=True) + jnp.sum(
            masses[1], axis=1, keepdims=True
        )
        attended = 0.0
        for side, kv in ((0, kv_own), (1, kv_other)):
            share = masses[side] / total
            prob[rows, pl.ds(side * 512, 512)] = share
            attended = attended + dot_nn(share.astype(BF16), kv[:, 256:512])
        attn[rows, :] = attended.astype(BF16)


ORDER = (2, 3, 1, 0)


def out_body(base, idx, *refs):
    weights = refs[:8]
    attn, act = refs[8:10]
    sends, keeps = refs[10:14], refs[14:18]
    w, sems = refs[18:]
    fills = place_inner(Copies(sems), weights, base, w, idx)
    x, z = idx[2], idx[3]
    finish(fills)
    for side, to in ((1, sends), (0, keeps)):
        rows = span(x if side == 0 else 1 - x, ROWS)
        for i, d in enumerate(ORDER):
            cols = span(z ^ d, WIDTH)
            value = dot_nn(attn[rows, :], w[0:256, cols]) + dot_nn(act[rows, :], w[256:1280, cols])
            to[i][...] = value.astype(to[i].dtype)


def add_body(kept, got, result):
    result[...] = (kept[...] + got[...].astype(F32)).astype(BF16)


def inner_grad(grad, weights, base, slope, outs, w, copies, idx, fills):
    g_attn, d_up, grad_sum, up_sum = outs
    grad_sum[...] = jnp.sum(grad[...].astype(F32), axis=0, keepdims=True)
    finish(fills)
    g_attn[...] = dot_nt(grad[...], w[0:256, :]).astype(BF16)
    for u in range(4):
        cols = pl.ds(u * 256, 256)
        value = (
            dot_nt(grad[...], w[pl.ds(256 + u * 256, 256), :]) * slope[:, cols]
        ).astype(BF16)
        d_up[:, cols] = value
        up_sum[0:1, cols] = jnp.sum(value.astype(F32), axis=0, keepdims=True)


def last_grad_body(base, idx, *refs):
    pieces, weights, slope = refs[:8], refs[8:16], refs[16]
    grad, outs = refs[17], refs[18:22]
    w, sems = refs[22:]
    copies = Copies(sems)
    loads = place_pieces(copies, pieces, grad, idx)
    fills = place_inner(copies, weights, base, w, idx)
    finish(loads)
    inner_grad(grad, weights, base, slope, outs, w, copies, idx, fills)


def next_grad_body(base, idx, *refs):
    pieces, weights, slope, later, xhat, inv_all = refs[:8], refs[8:16], *refs[16:20]
    grad, grad_piece, outs = refs[20], refs[21], refs[22:26]
    total, w, sems = refs[26:]
    copies = Copies(sems)
    loads = place_pieces(copies, pieces, total, idx)
    fills = place_inner(copies, weights, base, w, idx)
    finish(loads)
    step = 32

    def rows_of(i, carry):
        rows = pl.ds(pl.multiple_of(i * step, step), step)
        value = total[rows, :].astype(F32)
        normed = xhat[rows, :].astype(F32)
        mean = jnp.mean(value, axis=1, keepdims=True)
        slant = jnp.mean(value * normed, axis=1, keepdims=True)
        value = inv_all[rows, 0:1] * (value - mean - normed * slant)
        grad[rows, :] = (later[rows, :].astype(F32) + value).astype(BF16)
        return carry

    lax.fori_loop(0, 2 * ROWS // step, rows_of, 0)
    grad_piece[...] = grad[span(idx[2], ROWS), span(idx[3], WIDTH)]
    inner_grad(grad, weights, base, slope, outs, w, copies, idx, fills)


def attend_back_body(q, kv_own, kv_other, prob, g_attn, d_q, keep, send, d_score, share):
    scaling = HD**-0.5
    step = 128
    for part in range(2 * ROWS // step):
        rows = pl.ds(part * step, step)
        weights = prob[rows, :]
        d_prob = [dot_nt(g_attn[rows, :], kv[:, 256:512]) for kv in (kv_own, kv_other)]
        halves = [weights[:, :512], weights[:, 512:]]
        delta = jnp.sum(halves[0] * d_prob[0], axis=1, keepdims=True) + jnp.sum(
            halves[1] * d_prob[1], axis=1, keepdims=True
        )
        total = 0.0
        for side, kv in ((0, kv_own), (1, kv_other)):
            value = (halves[side] * (d_prob[side] - delta)).astype(BF16)
            d_score[rows, pl.ds(side * 512, 512)] = value
            total = total + dot_nn(value, kv[:, 0:256])
        d_q[rows, :] = total * scaling
        share[rows, :] = weights.astype(BF16)
    keep[:, 0:256] = dot_tn(d_score[:, 0:512], q[...]) * scaling
    keep[:, 256:512] = dot_tn(share[:, 0:512], g_attn[...])
    send[:, 0:256] = (dot_tn(d_score[:, 512:1024], q[...]) * scaling).astype(BF16)
    send[:, 256:512] = dot_tn(share[:, 512:1024], g_attn[...]).astype(BF16)


def outer_u_body(idx, n_one, d_up, keep, send):
    s, c = idx[0], pl.program_id(0)
    for k, to in ((1 - s, send), (s, keep)):
        value = dot_tn(n_one[:, span(2 * c + k, 256)], d_up[...]).astype(BF16)
        for u in range(4):
            to[0, u * 256 : (u + 1) * 256, :] = value[:, u * 256 : (u + 1) * 256]


def outer_o_body(idx, attn, act, grad, keep, send):
    s, c = idx[0], pl.program_id(0)
    g_cols = grad[:, span(c, WIDTH)]
    for k, to in ((1 - s, send), (s, keep)):
        value = dot_tn(attn[:, span(k, 128)], g_cols).astype(BF16)
        to[0, 0:128, :] = value[:, :256]
        to[0, 128:256, :] = value[:, 256:]
        value = dot_tn(act[:, span(k, 512)], g_cols).astype(BF16)
        to[0, 256:768, :] = value[:, :256]
        to[0, 768:1280, :] = value[:, 256:]


def outer_a_body(idx, n_zero, d_mix, keep, send):
    s, c = idx[0], pl.program_id(0)
    for k, to in ((1 - s, send), (s, keep)):
        value = dot_tn(n_zero[:, span(2 * c + k, 256)], d_mix[...]).astype(BF16)
        for t in range(3):
            to[0, t * 256 : (t + 1) * 256, :] = value[:, t * 256 : (t + 1) * 256]


class Part:
    def __init__(self, ref, k, base):
        self.ref, self.k, self.base = ref, k, base

    def __setitem__(self, at, value):
        rows = pl.ds(self.base + at[1].start, at[1].stop - at[1].start)
        self.ref[self.k, 0, 0, rows, :] = value


def outer_uo_body(idx, n_one, d_up, attn, act, grad, result, base=0):
    s = idx[0]
    outer_u_body(idx, n_one, d_up, Part(result, s, base), Part(result, 1 - s, base))
    base = base + U_ROWS
    outer_o_body(idx, attn, act, grad, Part(result, s, base), Part(result, 1 - s, base))


def outer_all_body(idx, n_zero, d_mix, *refs):
    s, result = idx[0], refs[5]
    outer_a_body(idx, n_zero, d_mix, Part(result, s, 0), Part(result, 1 - s, 0))
    outer_uo_body(idx, *refs, base=A_ROWS)


def outer(body, name, idx, ins, rows):
    if rows == A_ROWS:
        outs = [jax.ShapeDtypeStruct((4, rows, 256), BF16)] * 2
        specs = [pl.BlockSpec((1, rows, 256), lambda c: (c, 0, 0))] * 2
    else:
        outs = jax.ShapeDtypeStruct((2, 2, 2, rows, 256), BF16)
        specs = pl.BlockSpec((2, 1, 1, rows, 256), lambda c: (0, c // 2, c % 2, 0, 0))
    return pl.pallas_call(
        body,
        grid=(4,),
        out_shape=outs,
        in_specs=[SMEM] + [pl.BlockSpec(v.shape, lambda c: (0, 0)) for v in ins],
        out_specs=specs,
        name=name,
        cost_estimate=pl.CostEstimate(flops=1, bytes_accessed=1, transcendentals=0),
        compiler_params=pltpu.CompilerParams(vmem_limit_bytes=48 * 2**20),
    )(idx, *ins)


def mix_grad_body(base_a, base_u, idx, *refs):
    a_weights, u_weights = refs[:8], refs[8:16]
    d_q, d_kv, d_kv_got, cosine, front, back, d_up, xhat, wide = refs[16:25]
    d_mix, mix_sum, norm_sum, stats = refs[25:29]
    sends, keeps = refs[29:33], refs[33:37]
    w_a, w_u, sums, sems = refs[37:]
    copies = Copies(sems)
    fills = place_qkv(copies, a_weights, base_a, w_a, idx)
    for group in place_up(copies, u_weights, base_u, w_u, idx):
        fills += group
    x, z = idx[2], idx[3]
    for half in range(2):
        rows = pl.ds(half * ROWS, ROWS)
        tables = (cosine[rows, :], front[rows, :], back[rows, :])
        got = d_kv_got[rows, :].astype(F32)
        total = d_kv[rows, :] + got
        d_mix[rows, 0:128] = turn(d_q[rows, 0:128], tables, -1.0).astype(BF16)
        d_mix[rows, 128:256] = d_q[rows, 128:256].astype(BF16)
        d_mix[rows, 256:384] = turn(total[:, 0:128], tables, -1.0).astype(BF16)
        d_mix[rows, 384:768] = total[:, 128:512].astype(BF16)
    mix_sum[...] = jnp.sum(d_mix[...].astype(F32), axis=0, keepdims=True)
    sums[...] = jnp.zeros_like(sums)
    finish(fills)
    for i, d in enumerate(ORDER):
        cols = span(z ^ d, WIDTH)
        columns = []
        for side in (1, 0):
            rows = span(x if side == 0 else 1 - x, ROWS)
            dn_zero = dot_nt(d_mix[rows, :], w_a[cols, :])
            dn_one = dot_nt(d_up[rows, :], w_u[cols, :])
            normed = xhat[rows, cols].astype(F32)
            mixed = dn_zero * wide[0:1, cols] + dn_one * wide[1:2, cols]
            sums[rows, 0:1] += jnp.sum(mixed, axis=1, keepdims=True)
            sums[rows, 1:2] += jnp.sum(mixed * normed, axis=1, keepdims=True)
            columns.append(
                [
                    jnp.sum(value, axis=0, keepdims=True)
                    for value in (dn_zero * normed, dn_one * normed, dn_zero, dn_one)
                ]
            )
            if side == 1:
                sends[i][...] = mixed.astype(BF16)
            else:
                keeps[i][...] = mixed
        for j in range(4):
            norm_sum[j : j + 1, cols] = columns[0][j] + columns[1][j]
    stats[...] = jnp.transpose(sums[...])[0:8, :]


def input_grad_body(idx, kept, got, far_a, far_b, far_c, stats, xhat, inv, grad, result):
    x = idx[2]
    rows = stats[:, span(x, ROWS)] * (1.0 / MODEL)
    columns = jnp.transpose(jnp.concatenate([rows] * 16, axis=0))
    total = kept[...] + got[...].astype(F32)
    total = total + far_a[...].astype(F32) + far_b[...].astype(F32) + far_c[...].astype(F32)
    normed = xhat[...].astype(F32)
    value = inv[span(x, ROWS), 0:1] * (total - columns[:, 0:1] - normed * columns[:, 1:2])
    result[...] = (grad[...].astype(F32) + value).astype(BF16)


def small_sums_body(idx, *refs):
    result = refs[8]
    x, z = idx[2], idx[3]
    result[...] = jnp.zeros_like(result)
    for l in range(2):
        norm, mix, up, grad = refs[4 * l : 4 * l + 4]
        first = 12 * l
        result[first : first + 4, :] = norm[:, span(z, WIDTH)]
        for d in (1, 2, 3):
            base = 16 + 8 * d + 4 * l
            result[base : base + 4, :] = norm[:, span(z ^ d, WIDTH)]
        for t in range(3):
            result[first + 4 + t : first + 5 + t, span(x, 256)] = mix[0:1, t * 256 : (t + 1) * 256]
        for half in range(2):
            result[pl.ds(first + 7 + 2 * x + half, 1), :] = up[0:1, half * 512 : (half + 1) * 512]
        result[first + 11 : first + 12, :] = jnp.where(x == 0, grad[0:1, span(z, WIDTH)], 0.0)


def unpack_a_body(idx, own, got, qkv):
    s, x = idx[0], idx[2]
    for k, pair in ((s, own), (1 - s, got)):
        for side, xx in ((0, x), (1, 1 - x)):
            for t in range(3):
                qkv[t, span(k, 256), span(xx, 256)] = pair[side, t * 256 : (t + 1) * 256, :].astype(F32)


def unpack_uo_body(idx, own, got, up, out, down):
    s, x = idx[0], idx[2]
    for k, pair in ((s, own), (1 - s, got)):
        for side, xx in ((0, x), (1, 1 - x)):
            for u in range(4):
                up[span(k, 256), span(xx * 4 + u, 256)] = pair[
                    side, u * 256 : (u + 1) * 256, :
                ].astype(F32)
            for half in range(2):
                cols = slice(half * 256, half * 256 + 256)
                first = U_ROWS + half * 128
                out[span(2 * xx + k, 128), cols] = pair[side, first : first + 128, :].astype(F32)
                first = U_ROWS + 256 + half * 512
                down[span(2 * xx + k, 512), cols] = pair[side, first : first + 512, :].astype(F32)


def after(value, *done):
    return lax.optimization_barrier((value, *done))[0]


def relay_shards(
    block_input,
    out_cotangent,
    doc_lengths,
    norm_gain,
    norm_bias,
    qkv_weight,
    qkv_bias,
    out_weight,
    out_bias,
    up_weight,
    up_bias,
    down_weight,
    down_bias,
):
    s = lax.axis_index("section")
    y = lax.axis_index("y")
    x = lax.axis_index("x")
    z = lax.axis_index("tensor")
    idx = jnp.stack([s, y, x, z]).astype(jnp.int32)
    dma = pltpu.SemaphoreType.DMA

    def spread_near(piece):
        near = [piece] + [None] * 3
        for d in (2, 3, 1):
            near[d] = across(piece, "tensor", d)
        return near

    def spread_far(near, *done):
        far = [None] * 4
        for d in (0, 2, 3, 1):
            far[d] = across(after(near[d], *done) if done else near[d], "x", 1)
        return near + far

    def spread(piece):
        return spread_far(spread_near(piece))

    def sum_over_x(sends):
        return [across(send, "x", 1) for send in sends]

    def added(keeps, got, i, *done):
        part = after(got[i], *done) if done else got[i]
        return call(
            add_body,
            "add_piece",
            (keeps[i], part),
            [VMEM] * 2,
            [((ROWS, WIDTH), BF16)],
            [VMEM],
            [],
        )[0]

    def sum_over_tensor(keeps, got, between=None, *done):
        totals = [added(keeps, got, i, *done) for i in range(2)]
        extra = None
        if between is not None:
            extra = between(totals)
        last = added(keeps, got, 2, *done, *([] if extra is None else jax.tree.leaves(extra)))
        far = [across(v, "tensor", d) for v, d in zip(totals + [last], ORDER)]
        return (far, extra) if between is not None else far

    def summed(keeps, got, far):
        total = keeps[3] + got[3].astype(F32)
        return total + far[0].astype(F32) + far[1].astype(F32) + far[2].astype(F32)

    to_piece = lambda ss, yy, xx, zz: (xx, ss, yy, zz)
    input_piece = routed(pick(block_input, s), to_piece)
    first = spread(input_piece)

    a_own, a_send = call(
        prepare_a_body,
        "prepare_a",
        (idx, qkv_weight[0].transpose(1, 0, 2)),
        [SMEM, VMEM],
        [((2, A_ROWS, 256), BF16)] * 2,
        [VMEM] * 2,
        [],
    )
    a_got = across(a_send, "section", 1)
    u_own, u_send, o_own, o_send = call(
        prepare_f_body,
        "prepare_f",
        (idx, out_weight[0], up_weight[0], down_weight[0]),
        [SMEM] + [VMEM] * 3,
        [((2, U_ROWS, 256), BF16)] * 2 + [((2, O_ROWS, 256), BF16)] * 2,
        [VMEM] * 4,
        [],
    )
    u_got = across(u_send, "section", 1)
    o_got = across(o_send, "section", 1)
    x_chain, y_chain = [], []

    def fetch(own, got, layer, x_done=(), m_done=(), r_done=(), k_done=()):
        mine, other = [jnp.where(s == layer, own[i], got[i]) for i in range(2)]
        other = after(other, *x_chain[-1:], *x_done)
        pieces = [mine, across(other, "x", 1)]
        x_chain.append(pieces[1])
        for value, done in ((mine, m_done), (pieces[1], r_done)):
            pieces.append(across(after(value, *y_chain[-2:-1], *done), "y", 1))
            y_chain.append(pieces[-1])
        bound = [after(v, *k_done) for v in pieces] if k_done else pieces
        return pieces + [across(v, "section", 1) for v in bound]

    small = jnp.concatenate(
        [norm_gain[0], norm_bias[0], out_bias, down_bias, qkv_bias[0], up_bias[0].reshape(4, WIDTH)],
        axis=0,
    )
    small = in_order(small, across(small, "section", 1), s)
    norms = small[:, :4].reshape(8, WIDTH)
    pair = in_order(norms, across(norms, "tensor", 2), z // 2)
    near = across(pair, "tensor", 1)
    quads = in_order(pair, near, z % 2, 1)
    wide = quads.transpose(2, 0, 1, 3).reshape(2, 4, MODEL).astype(F32)
    bias_qkv = pick(small[:, 6:9].reshape(2, 3, 2, HD), x, 2).reshape(2, 1, 3 * HD).astype(F32)
    bias_up = pick(small[:, 9:].reshape(2, 2, HID), x, 1).reshape(2, 1, HID).astype(F32)
    bias_piece = small[:, 4:5].astype(F32) + small[:, 5:6].astype(F32)

    rows = jnp.arange(ROWS, dtype=jnp.int32)
    own_pos = jnp.concatenate([(2 * i + s) * ROWS + rows for i in range(2)])
    _, doc_pos = doc_layout(pick(doc_lengths, y), own_pos)
    cosine, sine = rotary_tables(doc_pos, ROT)
    cosine, sine = cosine[:, 0], sine[:, 0]
    blank = jnp.zeros((2 * ROWS, 32), F32)
    ones = jnp.ones((2 * ROWS, 64), F32)
    tables = (
        jnp.concatenate([cosine, cosine, ones], axis=1),
        jnp.concatenate([-sine, blank, blank, blank], axis=1),
        jnp.concatenate([blank, sine, blank, blank], axis=1),
    )
    full = (2 * ROWS, MODEL)

    wa_zero = fetch(a_own, a_got, 0)
    wu_zero = fetch(u_own, u_got, 0, (first[5],))

    def norm(layer, pieces, w_a, base):
        return call(
            functools.partial(norm_body, base),
            "norm_qkv",
            (idx, *pieces, *w_a, wide[layer], bias_qkv[layer], *tables),
            [SMEM] + [ANY] * 16 + [VMEM] * 5,
            [
                (full, BF16),
                (full, BF16),
                (full, BF16),
                ((512, 256), BF16),
                ((512, 512), BF16),
                ((ROWS, WIDTH), BF16),
                ((512, 128), F32),
            ],
            [VMEM] * 7,
            [
                pltpu.VMEM(full, BF16),
                pltpu.VMEM((MODEL, 768), BF16),
                dma((32,)),
            ],
        )

    def upward(layer, n_one, w_u, base):
        return call(
            functools.partial(up_body, base),
            "up_gelu",
            (idx, *w_u, n_one, bias_up[layer]),
            [SMEM] + [ANY] * 8 + [VMEM] * 2,
            [((512, HID), BF16), ((512, HID), F32)],
            [VMEM] * 2,
            [pltpu.VMEM((MODEL, HID), BF16), dma((32,))],
        )

    def attend(q, kv, kv_other):
        return call(
            attend_body,
            "attend",
            (idx, doc_lengths, q, kv, kv_other),
            [SMEM] * 2 + [VMEM] * 3,
            [((512, 1024), F32), ((512, 256), BF16)],
            [VMEM] * 2,
            [],
        )

    def downward(attn, act, w_o, base):
        parts = call(
            functools.partial(out_body, base),
            "out_down",
            (idx, *w_o, attn, act),
            [SMEM] + [ANY] * 8 + [VMEM] * 2,
            [((ROWS, WIDTH), BF16)] * 4 + [((ROWS, WIDTH), F32)] * 4,
            [VMEM] * 8,
            [pltpu.VMEM((1280, MODEL), BF16), dma((32,))],
        )
        return parts[:4], parts[4:]

    def state_of(layer, piece, total):
        return (piece.astype(F32) + total + bias_piece[layer]).astype(BF16)

    inner_outs = [
        ((512, 256), BF16),
        ((512, HID), BF16),
        ((1, MODEL), F32),
        ((1, HID), F32),
    ]

    def attend_back(q, kv, kv_other, prob, g_attn):
        return call(
            attend_back_body,
            "attend_back",
            (q, kv, kv_other, prob, g_attn),
            [VMEM] * 5,
            [((512, 256), F32), ((512, 512), F32), ((512, 512), BF16)],
            [VMEM] * 3,
            [pltpu.VMEM((512, 1024), BF16), pltpu.VMEM((512, 1024), BF16)],
        )

    def mix_grad(layer, d_q, d_kv, d_kv_got, d_up, xhat, w_a, w_u, bases):
        outs = call(
            functools.partial(mix_grad_body, *bases),
            "grad_mix",
            (idx, *w_a, *w_u, d_q, d_kv, d_kv_got, *tables, d_up, xhat, wide[layer]),
            [SMEM] + [ANY] * 16 + [VMEM] * 9,
            [((512, 768), BF16), ((1, 768), F32), ((4, MODEL), F32), ((8, 512), F32)]
            + [((ROWS, WIDTH), BF16)] * 4
            + [((ROWS, WIDTH), F32)] * 4,
            [VMEM] * 12,
            [
                pltpu.VMEM((MODEL, 768), BF16),
                pltpu.VMEM((MODEL, HID), BF16),
                pltpu.VMEM((512, 128), F32),
                dma((64,)),
            ],
        )
        return outs[:4], outs[4:8], outs[8:]

    def over_cores(pair):
        keep, send = pair
        got = across(send, "section", 1)
        shape = (2, 2) + keep.shape[1:]
        return keep.reshape(shape), got.reshape(shape)

    def summed_rows(grad):
        total = lax.psum_scatter(
            grad.reshape((4,) + grad.shape[2:]), ("section", "y"), scatter_dimension=0, tiled=True
        )
        return total[0], grad

    def y_part(keep, got):
        return (pick(keep, 1 - y).astype(F32) + pick(got, 1 - y).astype(F32)).astype(BF16)

    def x_part(keep, got, y_got, xx):
        at = lambda value: pick(pick(value, y), xx).astype(F32)
        return (at(keep) + at(got) + pick(y_got, xx).astype(F32)).astype(BF16)

    n_zero0, n_one0, xhat0, q0, kv0, x_piece0, inv0 = norm(0, first, wa_zero, 0)
    kv_other0 = across(kv0, "section", 1)
    cotangent_piece = routed(pick(out_cotangent, s), to_piece)
    act0, slope0 = upward(0, n_one0, wu_zero, 0)
    prob0, attn0 = attend(q0, kv0, kv_other0)
    wo_zero = fetch(o_own, o_got, 0, (kv0,), (kv0,), (act0,))
    wa_one = fetch(a_own, a_got, 1, (kv0,), (act0,), ())
    sends, keeps = downward(attn0, act0, wo_zero, 0)
    got = sum_over_x(sends)
    wu_one = fetch(u_own, u_got, 1, (act0,), (sends[0],), (got[0],))
    far = sum_over_tensor(keeps, got)
    state_zero = state_of(0, input_piece, summed(keeps, got, far))
    wo_one = fetch(o_own, o_got, 1, (got[3],), (state_zero,), (state_zero,))
    second = spread(state_zero)

    n_zero1, n_one1, xhat1, q1, kv1, _, inv1 = norm(1, second, wa_one, 0)
    kv_other1 = across(kv1, "section", 1)
    last_grad = spread_far(spread_near(after(cotangent_piece, kv0)), n_one1)
    act1, slope1 = upward(1, n_one1, wu_one, 0)
    prob1, attn1 = attend(q1, kv1, kv_other1)
    sends1, keeps1 = downward(attn1, act1, wo_one, 0)
    state_got = sum_over_x(sends1)

    grad1, g_attn1, d_up1, grad_sum1, up_sum1 = call(
        functools.partial(last_grad_body, 0),
        "last_grad",
        (idx, *last_grad[:7], after(last_grad[7], sends1[0]), *wo_one, slope1),
        [SMEM] + [ANY] * 16 + [VMEM],
        [(full, BF16)] + inner_outs,
        [VMEM] * 5,
        [pltpu.VMEM((1280, MODEL), BF16), dma((40,))],
    )
    d_q, d_kv, d_kv_send = attend_back(q1, kv1, kv_other1, prob1, g_attn1)
    d_kv_got = across(d_kv_send, "section", 1)
    uo_grad = outer(
        outer_uo_body,
        "outer_uo",
        idx,
        (n_one1, after(d_up1, d_q), attn1, act1, grad1),
        U_ROWS + O_ROWS,
    )
    (d_mix1, mix_sum1, norm_sum1, _), sends, keeps = mix_grad(
        1,
        after(d_q, uo_grad, *state_got),
        d_kv,
        d_kv_got,
        d_up1,
        xhat1,
        wa_one,
        wu_one,
        (0, 0),
    )
    uo_one, _ = summed_rows(after(uo_grad, norm_sum1))
    got = sum_over_x(sends)
    far = sum_over_tensor(keeps, got)
    mixed_piece = summed(keeps, got, far).astype(BF16)
    mixed = spread(mixed_piece)

    grad0, grad_one_piece, g_attn0, d_up0, grad_sum0, up_sum0 = call(
        functools.partial(next_grad_body, 0),
        "next_grad",
        (idx, *mixed, *wo_zero, slope0, grad1, xhat1, inv1),
        [SMEM] + [ANY] * 16 + [VMEM] * 4,
        [(full, BF16), ((ROWS, WIDTH), BF16)] + inner_outs,
        [VMEM] * 6,
        [pltpu.VMEM(full, BF16), pltpu.VMEM((1280, MODEL), BF16), dma((40,))],
    )
    both_grad = outer(
        outer_all_body,
        "outer_all",
        idx,
        (n_zero1, d_mix1, n_one0, d_up0, attn0, act0, grad0),
        A_ROWS + U_ROWS + O_ROWS,
    )
    both_sum, _ = summed_rows(after(both_grad, uo_one))
    d_q, d_kv, d_kv_send = attend_back(q0, kv0, kv_other0, prob0, after(g_attn0, both_grad))
    d_kv_got = across(d_kv_send, "section", 1)
    (d_mix0, mix_sum0, norm_sum0, stats), sends, keeps = mix_grad(
        0,
        d_q,
        d_kv,
        d_kv_got,
        d_up0,
        xhat0,
        wa_zero,
        wu_zero,
        (0, 0),
    )
    got = sum_over_x(sends)
    (sums,) = call(
        small_sums_body,
        "small_sums",
        (
            idx,
            norm_sum0,
            mix_sum0,
            up_sum0,
            grad_sum0,
            norm_sum1,
            mix_sum1,
            up_sum1,
            grad_sum1,
        ),
        [SMEM] + [VMEM] * 8,
        [((48, WIDTH), F32)],
        [VMEM],
        [],
    )
    sums_far = [across(sums[16 + 8 * d : 24 + 8 * d], "tensor", d) for d in (1, 2, 3)]
    for bits in (1, 2):
        stats = stats + across(stats, "tensor", bits)
    sums_far = (sums_far[0] + sums_far[1] + sums_far[2]).reshape(2, 4, WIDTH)
    sums = sums[:24].reshape(2, 12, WIDTH) + jnp.pad(sums_far, ((0, 0), (0, 8), (0, 0)))
    sums = jnp.concatenate([sums.reshape(24, WIDTH), stats], axis=0)
    totals = [added(keeps, got, i) for i in range(3)]
    far = [across(v, "tensor", d) for v, d in zip(totals, ORDER)]
    uo_one = after(uo_one, *got)
    uo_send = pick(uo_one, 1 - x)
    uo_x = across(uo_send, "x", 1)
    uo_one = (pick(uo_one, x), uo_x)
    a_grad = outer(outer_a_body, "outer_a", idx, (after(n_zero0, uo_x, *far), d_mix0), A_ROWS)
    a_sum = over_cores(a_grad)
    sums = sums + across(after(sums, *totals), "x", 1)
    sums, stats = sums[:24].reshape(2, 12, WIDTH), sums[24:]
    a_part = y_part(a_sum[0], after(a_sum[1], stats))
    sums_y = across(after(sums, a_part), "y", 1)
    a_y = across(a_part, "y", 1)
    state_far = sum_over_tensor(keeps1, state_got, None, uo_send)
    (grad_zero_piece,) = call(
        input_grad_body,
        "input_grad",
        (idx, keeps[3], got[3], *far, stats, x_piece0, inv0, grad_one_piece),
        [SMEM] + [VMEM] * 9,
        [((ROWS, WIDTH), BF16)],
        [VMEM],
        [],
    )
    both_sum = after(both_sum, uo_x, grad_zero_piece, a_part)
    both = (pick(both_sum, x), across(pick(both_sum, 1 - x), "x", 1))
    sums = sums + sums_y
    sums = pick(sums, s) + across(pick(sums, 1 - s), "section", 1)
    state_far[2] = after(state_far[2], a_y, sums_y)
    state_one = state_of(1, state_zero, summed(keeps1, state_got, state_far))
    a_zero = (x_part(*a_sum, a_y, x), across(x_part(*a_sum, a_y, 1 - x), "x", 1))

    for_zero = jnp.stack([state_zero, grad_zero_piece])
    for_one = jnp.stack([state_one, grad_one_piece])
    to_same = routed(
        jnp.where(y == 0, for_zero, for_one), lambda ss, yy, xx, zz: (yy, xx, ss, zz)
    )
    to_other = routed(
        jnp.where(y == 0, for_one, for_zero), lambda ss, yy, xx, zz: (1 - yy, xx, ss, zz)
    )
    placed = in_order(to_same, to_other, s, 1)

    both = after(both, placed)

    def unpacked(body, name, zero, one, shapes):
        zero, one = jnp.stack(zero), jnp.stack(one)
        own = jnp.where(s == 0, zero, one)
        got = across(jnp.where(s == 0, one, zero), "section", 1)
        return call(
            body,
            name,
            (idx, own, got),
            [SMEM] + [VMEM] * 2,
            [(shape, F32) for shape in shapes],
            [VMEM] * len(shapes),
            [],
        )

    out_up, out_out, out_down = unpacked(
        unpack_uo_body,
        "unpack_uo",
        [v[A_ROWS:] for v in both],
        uo_one,
        [(WIDTH, 2 * HID), (WIDTH, WIDTH), (2 * HID, WIDTH)],
    )
    (out_qkv,) = unpacked(
        unpack_a_body, "unpack_a", a_zero, [v[:A_ROWS] for v in both], [(3, WIDTH, WIDTH)]
    )
    return (
        placed[0][None],
        placed[1][None],
        sums[None, 0:2],
        sums[None, 2:4],
        out_qkv.transpose(1, 0, 2)[None],
        sums[None, 4:7],
        out_out[None],
        sums[11:12],
        out_up[None],
        sums[7:11].reshape(1, 2 * HID),
        out_down[None],
        sums[11:12],
    )


def solution(mesh):
    sizes = dict(mesh.shape)
    body, ctx = shards, "ctx"
    if (sizes["section"], sizes["ctx"], sizes["tensor"]) == (2, 4, 4):
        body = relay_shards
        devices = mesh.devices.reshape(2, 2, 2, 4)
        mesh = jax.sharding.Mesh(devices, ("section", "y", "x", "tensor"))
        ctx = ("y", "x")
    in_specs = (
        P(None, ctx, "tensor"),
        P(None, ctx, "tensor"),
        P(),
        P("section", None, "tensor"),
        P("section", None, "tensor"),
        P("section", ctx, None, "tensor"),
        P("section", None, "tensor"),
        P("section", "tensor", ctx),
        P("section", "tensor"),
        P("section", ctx, "tensor"),
        P("section", "tensor"),
        P("section", "tensor", ctx),
        P("section", "tensor"),
    )
    out_specs = (
        P("section", None, ctx, "tensor"),
        P("section", None, ctx, "tensor"),
        P("section", None, "tensor"),
        P("section", None, "tensor"),
        P("section", ctx, None, "tensor"),
        P("section", None, "tensor"),
        P("section", "tensor", ctx),
        P("section", "tensor"),
        P("section", ctx, "tensor"),
        P("section", "tensor"),
        P("section", "tensor", ctx),
        P("section", "tensor"),
    )
    return jax.shard_map(body, mesh=mesh, in_specs=in_specs, out_specs=out_specs, check_vma=False)
```
